768 devices in a mesh: feat: 16 (over x_hi, y), batch: 24 (over x_lo, z), twin: 2 (over core).
Axes of the slice: x: 4 (x_hi: 2, x_lo: 2; x = x_hi * 2 + x_lo), y: 8, z: 12, core: 2. Of those that a mesh axis runs over, the one named last changes fastest.
Arguments:
- hidden_act: bfloat16 [2, 3072, 8192], P('twin', 'batch'), as said below
- proj_weight: bfloat16 [8192, 4608], P(None, 'feat'), may hold values from -0.0625 to 0.0625
Outputs:
- grad_normed: float32 [4608, 2, 3072], P(('feat', 'twin'), None, 'batch')
The draws below stay inside these ranges and needn't reach their ends.
Inputs may be any that keep to these rules, and one draw needn't show every extreme that they name: `hidden_act`: row r of both views is the same sample.
All inputs are finite; a program needn't handle non-finite values.
Results may differ from the reference program's by a relative error of at most 0.012.
The reference program's roundings to bfloat16 on the way count: a program that leaves them out, or rounds other values in their place, can miss the bound.
Values may be sent and summed in bfloat16 or wider, within the bound.
No kernel may reach another device: no remote copies, remote signals or barrier semaphores. Data moves between devices by JAX's collectives and lax.ppermute only.
A program may use at most 64 MiB of HBM per device.

```python
import math
import jax
import jax.numpy as jnp
from jax import lax

F = 4608
DH = 8192
TOKENS = 3072


view_link = 0.98


def draw_hidden_act(key, part):
    keys = jax.random.split(key, 4)
    row_ramp = 1.0 + 2.0 * jnp.arange(TOKENS, dtype=jnp.float32) / max(TOKENS - 1, 1)
    row_ramp = row_ramp[:, None]
    noise_first = jax.random.normal(keys[0], (TOKENS, DH), jnp.float32)
    noise_second = jax.random.normal(keys[1], (TOKENS, DH), jnp.float32)
    col_offset = 0.5 * jax.random.normal(keys[3], (1, DH), jnp.float32)
    row_scale = row_ramp
    mixing = math.sqrt(1.0 - view_link * view_link)
    first_view = col_offset + row_scale * noise_first
    second_view = col_offset + row_scale * (view_link * noise_first + mixing * noise_second)
    return jnp.stack([first_view, second_view], axis=0).astype(jnp.bfloat16)


def levels(own_key, dims, shards, smallest, top_value):
    def one(dim, shards_of):
        draws = jax.random.uniform(jax.random.fold_in(jax.random.fold_in(own_key, 6), dim), (shards_of,), jnp.float32, smallest / len(shards), top_value / len(shards))
        return jnp.repeat(jnp.exp(draws), dims[dim] // shards_of).reshape((-1,) + (1,) * (len(dims) - dim - 1))

    gain = one(*shards[0])
    for cut in shards[1:]:
        gain = gain * one(*cut)
    return gain


def centred(own_key, shape, width, bound, pieces=(), held_as=jnp.bfloat16):
    values = width * jax.random.normal(own_key, shape, jnp.float32)
    if pieces:
        values = values * levels(own_key, shape, pieces, -0.22, 0.18)
    return jnp.clip(values, -bound, bound).astype(held_as)


def setup_inputs(seed: int = 0) -> dict:
    splits = jax.random.split(jax.random.key(seed), 3)
    return {
        "hidden_act": draw_hidden_act(jax.random.fold_in(splits[2], 71), 0),
        "proj_weight": centred(splits[1], (DH, F), DH ** -0.5, 0.0625, ((1, 16),)),
    }


epsilon = 1e-05
off_weight = 0.0051

def wide_dot(left, right):
    return jnp.dot(left.astype(jnp.float32), right.astype(jnp.float32), precision=lax.Precision.HIGHEST, preferred_element_type=jnp.float32)

def normalize(view_rows, proj_weight):
    projected = wide_dot(view_rows, proj_weight).T
    row_total = projected.shape[1]
    feat_mean = lax.optimization_barrier(jnp.sum(projected, axis=1, keepdims=True)) / row_total
    feat_var = lax.optimization_barrier(jnp.sum(projected * projected, axis=1, keepdims=True)) / row_total - feat_mean * feat_mean
    return ((projected - feat_mean) * lax.rsqrt(feat_var + epsilon)).astype(jnp.bfloat16)

def reference(hidden_act, proj_weight):
    first_view = normalize(hidden_act[0], proj_weight)
    second_view = normalize(hidden_act[1], proj_weight)
    row_total = first_view.shape[1]
    corr = wide_dot(first_view, second_view.T) / row_total
    diagonal = jnp.eye(corr.shape[0], dtype=bool)
    grad_corr = jnp.where(diagonal, -2.0 * (1.0 - corr), 2.0 * off_weight * corr).astype(jnp.bfloat16)
    grad_first = wide_dot(grad_corr, second_view)
    grad_second = wide_dot(grad_corr.T, first_view)
    return jnp.stack([grad_first, grad_second], axis=1)
```

```python
import jax
import jax.numpy as jnp
from jax import lax
from jax.sharding import Mesh
from jax.sharding import PartitionSpec as P

epsilon = 1e-05
off_weight = 0.0051
batch_axes = ("x_lo", "z")
feat_axes = ("x_hi", "y")
bf16, f32 = jnp.bfloat16, jnp.float32


def spread(part, axes):
    copies = jnp.broadcast_to(part[None], (lax.axis_size(axes),) + part.shape)
    return lax.all_to_all(copies, axes, 0, 0, tiled=True)


def shards(hidden_act, proj_weight):
    batches, feats = lax.axis_size(batch_axes), lax.axis_size(feat_axes)
    view_rows = hidden_act[0]
    rows_here = view_rows.shape[0]
    row_total = rows_here * batches
    feat_here = proj_weight.shape[1]
    own = feat_here // batches
    batch_index, feat_index = lax.axis_index(batch_axes), lax.axis_index(feat_axes)
    twin = lax.axis_index("twin")
    projected = lax.dot_general(
        proj_weight, view_rows, (((0,), (1,)), ((), ())), preferred_element_type=f32
    )
    projected = lax.optimization_barrier(projected)
    by_rows = lax.all_to_all(
        projected.reshape(batches, own, rows_here), batch_axes, 0, 0, tiled=True
    )
    feat_mean = jnp.sum(by_rows, axis=(0, 2), keepdims=True) / row_total
    squares = jnp.sum(by_rows * by_rows, axis=(0, 2), keepdims=True) / row_total
    feat_var = squares - feat_mean * feat_mean
    normed = ((by_rows - feat_mean) * lax.rsqrt(feat_var + epsilon)).astype(bf16)
    normed = normed.transpose(1, 0, 2).reshape(own, row_total)
    other = lax.ppermute(normed, "twin", [(0, 1), (1, 0)])
    both = lax.ppermute(normed, "x_lo", [(0, 1), (1, 0)])
    low = lax.axis_index("x_lo") == 0
    pair = jnp.stack([jnp.where(low, normed, both), jnp.where(low, both, normed)])
    here = lax.all_gather(pair, "z", axis=1)
    there = spread(other, feat_axes)
    here = here.reshape(batches * own, row_total)
    there = there.reshape(feats * own, row_total)
    corr = lax.dot_general(
        here, there, (((1,), (1,)), ((), ())), preferred_element_type=f32
    ) / row_total
    row_ids = lax.broadcasted_iota(jnp.int32, corr.shape, 0) + feat_index * feat_here
    cols = lax.broadcasted_iota(jnp.int32, corr.shape, 1)
    col_ids = (cols // own) * feat_here + batch_index * own + cols % own
    grad = jnp.where(
        row_ids == col_ids, -2.0 * (1.0 - corr), 2.0 * off_weight * corr
    ).astype(bf16)
    part = jnp.einsum(
        "ij,jbr->bir",
        grad,
        there.reshape(feats * own, batches, rows_here),
        preferred_element_type=f32,
    ).astype(bf16)
    terms = lax.all_to_all(part, batch_axes, 0, 0, tiled=True)
    total = jnp.sum(terms.astype(f32), axis=0)
    first, second = jnp.split(total, 2, axis=0)
    keep = jnp.where(twin == 0, first, second)
    give = jnp.where(twin == 0, second, first)
    take = lax.ppermute(give, "twin", [(0, 1), (1, 0)])
    return jnp.stack(
        [jnp.where(twin == 0, keep, take), jnp.where(twin == 0, take, keep)], axis=1
    )


def solution(mesh):
    x_parts = 2
    shape = mesh.devices.shape
    fine = Mesh(
        mesh.devices.reshape(
            x_parts, shape[0] // x_parts, x_parts, shape[1] // x_parts, shape[2]
        ),
        ("x_hi", "y", "x_lo", "z", "twin"),
    )
    return jax.shard_map(
        shards,
        mesh=fine,
        in_specs=(P("twin", batch_axes, None), P(None, feat_axes)),
        out_specs=P(feat_axes + ("twin",), None, batch_axes),
        check_vma=False,
    )
```

```python
import jax
import jax.numpy as jnp
from jax import lax
from jax.experimental import pallas as pl
from jax.experimental.pallas import tpu as pltpu
from jax.sharding import Mesh
from jax.sharding import PartitionSpec as P

epsilon = 1e-05
off_weight = 0.0051
batch_axes = ("x_lo", "z")
feat_axes = ("x_hi", "y")
bf16, f32 = jnp.bfloat16, jnp.float32
swap = [(0, 1), (1, 0)]


def spread(part, axes):
    copies = jnp.broadcast_to(part[None], (lax.axis_size(axes),) + part.shape)
    return lax.all_to_all(copies, axes, 0, 0, tiled=True)


def product_kernel(grad_ref, other_ref, out_ref):
    rows_here = out_ref.shape[2]
    for block in range(out_ref.shape[0]):
        out_ref[block] = jnp.dot(
            grad_ref[...],
            other_ref[:, block * rows_here : (block + 1) * rows_here],
            preferred_element_type=f32,
        ).astype(bf16)


def products(grad, other, rows_here):
    blocks = other.shape[1] // rows_here
    return pl.pallas_call(
        product_kernel,
        out_shape=jax.ShapeDtypeStruct((blocks, grad.shape[0], rows_here), bf16),
        in_specs=[pl.BlockSpec(memory_space=pltpu.VMEM)] * 2,
        out_specs=pl.BlockSpec(memory_space=pltpu.VMEM),
        compiler_params=pltpu.CompilerParams(vmem_limit_bytes=24 * 2**20),
    )(grad, other)


def shards(hidden_act, proj_weight):
    depth = lax.axis_size("z")
    view_rows = hidden_act[0]
    rows_here = view_rows.shape[0]
    half_rows = rows_here * depth
    row_total = half_rows * lax.axis_size("x_lo")
    feat_here = proj_weight.shape[1]
    own = feat_here // depth
    twin = lax.axis_index("twin")
    projected = lax.dot_general(
        proj_weight, view_rows, (((0,), (1,)), ((), ())), preferred_element_type=f32
    )
    projected = lax.optimization_barrier(projected)
    by_rows = lax.all_to_all(
        projected.reshape(depth, own, rows_here), "z", 0, 0, tiled=True
    )
    sums = jnp.stack(
        [jnp.sum(by_rows, axis=(0, 2)), jnp.sum(by_rows * by_rows, axis=(0, 2))]
    )
    sums = sums + lax.ppermute(sums, "x_lo", swap)
    feat_mean = (sums[0] / row_total)[None, :, None]
    feat_var = (sums[1] / row_total)[None, :, None] - feat_mean * feat_mean
    normed = ((by_rows - feat_mean) * lax.rsqrt(feat_var + epsilon)).astype(bf16)
    normed = normed.transpose(1, 0, 2).reshape(own, half_rows)
    far = lax.ppermute(normed, "x_hi", swap)
    other = lax.ppermute(normed, "twin", swap)
    low = lax.axis_index("x_hi") == 0
    pair = jnp.concatenate([jnp.where(low, normed, far), jnp.where(low, far, normed)])
    there = lax.all_gather(pair, "y", axis=0, tiled=True)
    here = spread(other, "z").reshape(feat_here, half_rows)
    corr = lax.dot_general(
        here, there, (((1,), (1,)), ((), ())), preferred_element_type=f32
    )
    corr = (corr + lax.ppermute(corr, "x_lo", swap)) / row_total
    row_ids = lax.broadcasted_iota(jnp.int32, corr.shape, 0)
    row_ids = row_ids + lax.axis_index(feat_axes) * feat_here
    cols = lax.broadcasted_iota(jnp.int32, corr.shape, 1)
    chunks = cols // own
    col_feats = (chunks % 2) * lax.axis_size("y") + chunks // 2
    col_ids = col_feats * feat_here + lax.axis_index("z") * own + cols % own
    grad = jnp.where(
        row_ids == col_ids, -2.0 * (1.0 - corr), 2.0 * off_weight * corr
    ).astype(bf16)
    terms = lax.all_to_all(products(grad, there, rows_here), "z", 0, 0, tiled=True)
    total = jnp.sum(terms.astype(f32), axis=0)
    first, second = jnp.split(total, 2, axis=0)
    keep = jnp.where(twin == 0, first, second)
    give = jnp.where(twin == 0, second, first)
    take = lax.ppermute(give, "twin", swap)
    return jnp.stack(
        [jnp.where(twin == 0, take, keep), jnp.where(twin == 0, keep, take)], axis=1
    )


def solution(mesh):
    parts = 2
    shape = mesh.devices.shape
    fine = Mesh(
        mesh.devices.reshape(
            parts, shape[0] // parts, parts, shape[1] // parts, shape[2]
        ),
        ("x_hi", "y", "x_lo", "z", "twin"),
    )
    return jax.shard_map(
        shards,
        mesh=fine,
        in_specs=(P("twin", batch_axes, None), P(None, feat_axes)),
        out_specs=P(feat_axes + ("twin",), None, batch_axes),
        check_vma=False,
    )
```

```python
import jax
import jax.numpy as jnp
from jax import lax
from jax.experimental import pallas as pl
from jax.experimental.pallas import tpu as pltpu
from jax.sharding import Mesh
from jax.sharding import PartitionSpec as P

epsilon = 1e-05
off_weight = 0.0051
batch_axes = ("x_lo", "z")
feat_axes = ("x_hi", "y")
bf16, f32 = jnp.bfloat16, jnp.float32
swap = [(0, 1), (1, 0)]


def spread(part, axes):
    copies = jnp.broadcast_to(part[None], (lax.axis_size(axes),) + part.shape)
    return lax.all_to_all(copies, axes, 0, 0, tiled=True)


def product_kernel(grad_ref, other_ref, out_ref):
    rows_here = out_ref.shape[2]
    for block in range(out_ref.shape[0]):
        out_ref[block] = jnp.dot(
            grad_ref[...],
            other_ref[:, block * rows_here : (block + 1) * rows_here],
            preferred_element_type=f32,
        ).astype(bf16)


def products(grad, other, rows_here):
    blocks = other.shape[1] // rows_here
    return pl.pallas_call(
        product_kernel,
        out_shape=jax.ShapeDtypeStruct((blocks, grad.shape[0], rows_here), bf16),
        in_specs=[pl.BlockSpec(memory_space=pltpu.VMEM)] * 2,
        out_specs=pl.BlockSpec(memory_space=pltpu.VMEM),
        compiler_params=pltpu.CompilerParams(vmem_limit_bytes=24 * 2**20),
    )(grad, other)


def shards(hidden_act, proj_weight):
    depth, feats = lax.axis_size("z"), lax.axis_size(feat_axes)
    view_rows = hidden_act[0]
    rows_here = view_rows.shape[0]
    half_rows = rows_here * depth
    row_total = half_rows * lax.axis_size("x_lo")
    feat_here = proj_weight.shape[1]
    own = feat_here // depth
    twin = lax.axis_index("twin")
    projected = lax.dot_general(
        proj_weight, view_rows, (((0,), (1,)), ((), ())), preferred_element_type=f32
    )
    projected = lax.optimization_barrier(projected)
    by_rows = lax.all_to_all(
        projected.reshape(depth, own, rows_here), "z", 0, 0, tiled=True
    )
    sums = jnp.stack(
        [jnp.sum(by_rows, axis=(0, 2)), jnp.sum(by_rows * by_rows, axis=(0, 2))]
    )
    sums = lax.psum(sums, "x_lo")
    feat_mean = (sums[0] / row_total)[None, :, None]
    feat_var = (sums[1] / row_total)[None, :, None] - feat_mean * feat_mean
    normed = ((by_rows - feat_mean) * lax.rsqrt(feat_var + epsilon)).astype(bf16)
    normed = normed.transpose(1, 0, 2).reshape(own, half_rows)
    other = lax.ppermute(normed, "twin", swap)
    there = spread(normed, feat_axes).reshape(feats * own, half_rows)
    here = lax.all_gather(other, "z", axis=0, tiled=True)
    corr = lax.dot_general(
        here, there, (((1,), (1,)), ((), ())), preferred_element_type=f32
    )
    corr = (corr + lax.ppermute(corr, "x_lo", swap)) / row_total
    row_ids = lax.broadcasted_iota(jnp.int32, corr.shape, 0)
    row_ids = row_ids + lax.axis_index(feat_axes) * feat_here
    cols = lax.broadcasted_iota(jnp.int32, corr.shape, 1)
    col_ids = (cols // own) * feat_here + lax.axis_index("z") * own + cols % own
    grad = jnp.where(
        row_ids == col_ids, -2.0 * (1.0 - corr), 2.0 * off_weight * corr
    ).astype(bf16)
    terms = lax.all_to_all(products(grad, there, rows_here), "z", 0, 0, tiled=True)
    total = jnp.sum(terms.astype(f32), axis=0)
    first, second = jnp.split(total, 2, axis=0)
    keep = jnp.where(twin == 0, first, second)
    give = jnp.where(twin == 0, second, first)
    take = lax.ppermute(give, "twin", swap)
    return jnp.stack(
        [jnp.where(twin == 0, take, keep), jnp.where(twin == 0, keep, take)], axis=1
    )


def solution(mesh):
    parts = 2
    shape = mesh.devices.shape
    fine = Mesh(
        mesh.devices.reshape(
            parts, shape[0] // parts, parts, shape[1] // parts, shape[2]
        ),
        ("x_hi", "y", "x_lo", "z", "twin"),
    )
    return jax.shard_map(
        shards,
        mesh=fine,
        in_specs=(P("twin", batch_axes, None), P(None, feat_axes)),
        out_specs=P(feat_axes + ("twin",), None, batch_axes),
        check_vma=False,
    )
```

```python
import jax
import jax.numpy as jnp
from jax import lax
from jax.experimental import pallas as pl
from jax.experimental.pallas import tpu as pltpu
from jax.sharding import Mesh
from jax.sharding import PartitionSpec as P

epsilon = 1e-05
off_weight = 0.0051
batch_axes = ("x_lo", "z")
feat_axes = ("x_hi", "y")
bf16, f32 = jnp.bfloat16, jnp.float32
swap = [(0, 1), (1, 0)]


def spread(part, axes):
    copies = jnp.broadcast_to(part[None], (lax.axis_size(axes),) + part.shape)
    return lax.all_to_all(copies, axes, 0, 0, tiled=True)


def project_kernel(weight_ref, rows_ref, out_ref):
    @pl.when(pl.program_id(0) == 0)
    def _():
        out_ref[...] = jnp.zeros_like(out_ref)

    out_ref[...] += lax.dot_general(
        weight_ref[...],
        rows_ref[...],
        (((1,), (1,)), ((), ())),
        preferred_element_type=f32,
    )


def project(weight, rows, steps=8):
    width = weight.shape[1] // steps
    return pl.pallas_call(
        project_kernel,
        grid=(steps,),
        out_shape=jax.ShapeDtypeStruct((weight.shape[0], rows.shape[0]), f32),
        in_specs=[
            pl.BlockSpec((weight.shape[0], width), lambda k: (0, k)),
            pl.BlockSpec((rows.shape[0], width), lambda k: (0, k)),
        ],
        out_specs=pl.BlockSpec((weight.shape[0], rows.shape[0]), lambda k: (0, 0)),
        compiler_params=pltpu.CompilerParams(vmem_limit_bytes=56 * 2**20),
    )(weight, rows)


def normalize(by_rows, sums, row_total):
    feat_mean = (sums[0] / row_total)[None, :, None]
    feat_var = (sums[1] / row_total)[None, :, None] - feat_mean * feat_mean
    normed = ((by_rows - feat_mean) * lax.rsqrt(feat_var + epsilon)).astype(bf16)
    return normed.transpose(1, 0, 2).reshape(by_rows.shape[1], -1)


def product_kernel(grad_ref, other_ref, out_ref):
    rows_here = out_ref.shape[2]
    for block in range(out_ref.shape[0]):
        out_ref[block] = jnp.dot(
            grad_ref[...],
            other_ref[:, block * rows_here : (block + 1) * rows_here],
            preferred_element_type=f32,
        ).astype(bf16)


def products(grad, other, rows_here):
    blocks = other.shape[1] // rows_here
    return pl.pallas_call(
        product_kernel,
        out_shape=jax.ShapeDtypeStruct((blocks, grad.shape[0], rows_here), bf16),
        in_specs=[pl.BlockSpec(memory_space=pltpu.VMEM)] * 2,
        out_specs=pl.BlockSpec(memory_space=pltpu.VMEM),
        compiler_params=pltpu.CompilerParams(vmem_limit_bytes=24 * 2**20),
    )(grad, other)


def shards(hidden_act, proj_weight):
    depth, feats = lax.axis_size("z"), lax.axis_size(feat_axes)
    view_rows = hidden_act[0]
    rows_here = view_rows.shape[0]
    half_rows = rows_here * depth
    row_total = half_rows * lax.axis_size("x_lo")
    feat_here = proj_weight.shape[1]
    own = feat_here // depth
    twin = lax.axis_index("twin")
    projected = project(proj_weight.T, view_rows)
    by_rows = lax.all_to_all(
        projected.reshape(depth, own, rows_here), "z", 0, 0, tiled=True
    )
    sums = jnp.stack(
        [jnp.sum(by_rows, axis=(0, 2)), jnp.sum(by_rows * by_rows, axis=(0, 2))]
    )
    normed = normalize(by_rows, lax.psum(sums, "x_lo"), row_total)
    normed, other = lax.optimization_barrier(
        (normed, lax.ppermute(normed, "twin", swap))
    )
    there = spread(normed, feat_axes).reshape(feats * own, half_rows)
    here = lax.all_gather(other, "z", axis=0, tiled=True)
    corr = lax.dot_general(
        here, there, (((1,), (1,)), ((), ())), preferred_element_type=f32
    )
    corr = (corr + lax.ppermute(corr, "x_lo", swap)) / row_total
    row_ids = lax.broadcasted_iota(jnp.int32, corr.shape, 0)
    row_ids = row_ids + lax.axis_index(feat_axes) * feat_here
    cols = lax.broadcasted_iota(jnp.int32, corr.shape, 1)
    col_ids = (cols // own) * feat_here + lax.axis_index("z") * own + cols % own
    grad = jnp.where(
        row_ids == col_ids, -2.0 * (1.0 - corr), 2.0 * off_weight * corr
    ).astype(bf16)
    terms = lax.all_to_all(products(grad, there, rows_here), "z", 0, 0, tiled=True)
    total = jnp.sum(terms.astype(f32), axis=0)
    first, second = jnp.split(total, 2, axis=0)
    keep = jnp.where(twin == 0, first, second)
    give = jnp.where(twin == 0, second, first)
    take = lax.ppermute(give, "twin", swap)
    return jnp.stack(
        [jnp.where(twin == 0, take, keep), jnp.where(twin == 0, keep, take)], axis=1
    )


def solution(mesh):
    parts = 2
    shape = mesh.devices.shape
    fine = Mesh(
        mesh.devices.reshape(
            parts, shape[0] // parts, parts, shape[1] // parts, shape[2]
        ),
        ("x_hi", "y", "x_lo", "z", "twin"),
    )
    return jax.shard_map(
        shards,
        mesh=fine,
        in_specs=(P("twin", batch_axes, None), P(None, feat_axes)),
        out_specs=P(feat_axes + ("twin",), None, batch_axes),
        check_vma=False,
    )
```

```python
import functools

import jax
import jax.numpy as jnp
from jax import lax
from jax.experimental import pallas as pl
from jax.experimental.pallas import tpu as pltpu
from jax.sharding import Mesh
from jax.sharding import PartitionSpec as P

epsilon = 1e-05
off_weight = 0.0051
batch_axes = ("x_lo", "z")
feat_axes = ("x_hi", "y")
bf16, f32 = jnp.bfloat16, jnp.float32
swap = [(0, 1), (1, 0)]


def spread(part, axes):
    copies = jnp.broadcast_to(part[None], (lax.axis_size(axes),) + part.shape)
    return lax.all_to_all(copies, axes, 0, 0, tiled=True)


def project_kernel(weight_hbm, rows_hbm, out_ref, weight_ref, rows_ref, sems):
    parts = sems.shape[1]
    width = weight_ref.shape[1] // parts
    copies = []
    for part in range(parts):
        cols = pl.ds(part * width, width)
        pair = [
            pltpu.make_async_copy(
                weight_hbm.at[:, cols], weight_ref.at[:, cols], sems.at[0, part]
            ),
            pltpu.make_async_copy(
                rows_hbm.at[:, cols], rows_ref.at[:, cols], sems.at[1, part]
            ),
        ]
        for copy in pair:
            copy.start()
        copies.append(pair)
    total = None
    for part, pair in enumerate(copies):
        for copy in pair:
            copy.wait()
        cols = slice(part * width, (part + 1) * width)
        term = lax.dot_general(
            weight_ref[:, cols],
            rows_ref[:, cols],
            (((1,), (1,)), ((), ())),
            preferred_element_type=f32,
        )
        total = term if total is None else total + term
    out_ref[...] = total


def project(weight, rows, parts=8):
    return pl.pallas_call(
        project_kernel,
        out_shape=jax.ShapeDtypeStruct((weight.shape[0], rows.shape[0]), f32),
        in_specs=[pl.BlockSpec(memory_space=pl.ANY)] * 2,
        out_specs=pl.BlockSpec(memory_space=pltpu.VMEM),
        scratch_shapes=[
            pltpu.VMEM(weight.shape, bf16),
            pltpu.VMEM(rows.shape, bf16),
            pltpu.SemaphoreType.DMA((2, parts)),
        ],
        compiler_params=pltpu.CompilerParams(vmem_limit_bytes=56 * 2**20),
    )(weight, rows)


def on_diagonal(place_ref, shape):
    rows = lax.broadcasted_iota(jnp.int32, shape, 0)
    cols = lax.broadcasted_iota(jnp.int32, shape, 1)
    top, left, own = place_ref[0], place_ref[1], place_ref[2]
    return (cols - rows == left - top) & (rows >= top) & (rows < top + own)


def pack_kernel(place_ref, corr_ref, packed_ref):
    corr = corr_ref[...]
    feats = corr.shape[0]
    diagonal = jnp.where(on_diagonal(place_ref, corr.shape), corr, 0.0)
    diagonal = jnp.sum(diagonal, axis=0, keepdims=True)
    high = diagonal.astype(bf16).astype(f32)
    middle = (diagonal - high).astype(bf16).astype(f32)
    low = diagonal - high - middle
    extra = packed_ref.shape[0] - feats
    index = lax.broadcasted_iota(jnp.int32, (extra, corr.shape[1]), 0)
    tail = jnp.where(index == 0, high, jnp.where(index == 1, middle, low))
    packed_ref[:feats] = corr.astype(bf16)
    packed_ref[feats:] = jnp.where(index < 3, tail, 0.0).astype(bf16)


def pack(place, corr):
    return pl.pallas_call(
        pack_kernel,
        out_shape=jax.ShapeDtypeStruct((corr.shape[0] + 16, corr.shape[1]), bf16),
        in_specs=[
            pl.BlockSpec(memory_space=pltpu.SMEM),
            pl.BlockSpec(memory_space=pltpu.VMEM),
        ],
        out_specs=pl.BlockSpec(memory_space=pltpu.VMEM),
        compiler_params=pltpu.CompilerParams(vmem_limit_bytes=24 * 2**20),
    )(place, corr)


def product_kernel(row_total, place_ref, corr_ref, taken_ref, other_ref, out_ref):
    feats = corr_ref.shape[0]
    rows_here = out_ref.shape[2]
    diagonal = on_diagonal(place_ref, corr_ref.shape)
    terms = jnp.sum(taken_ref[feats:].astype(f32), axis=0, keepdims=True)
    taken = jnp.where(diagonal, terms, taken_ref[:feats].astype(f32))
    corr = (corr_ref[...] + taken) / row_total
    grad = jnp.where(diagonal, -2.0 * (1.0 - corr), 2.0 * off_weight * corr)
    grad = grad.astype(bf16)
    for block in range(out_ref.shape[0]):
        out_ref[block] = jnp.dot(
            grad,
            other_ref[:, block * rows_here : (block + 1) * rows_here],
            preferred_element_type=f32,
        ).astype(bf16)


def products(place, corr, taken, other, rows_here, row_total):
    blocks = other.shape[1] // rows_here
    return pl.pallas_call(
        functools.partial(product_kernel, row_total),
        out_shape=jax.ShapeDtypeStruct((blocks, corr.shape[0], rows_here), bf16),
        in_specs=[pl.BlockSpec(memory_space=pltpu.SMEM)]
        + [pl.BlockSpec(memory_space=pltpu.VMEM)] * 3,
        out_specs=pl.BlockSpec(memory_space=pltpu.VMEM),
        compiler_params=pltpu.CompilerParams(vmem_limit_bytes=24 * 2**20),
    )(place, corr, taken, other)


def shards(hidden_act, proj_weight):
    depth, feats = lax.axis_size("z"), lax.axis_size(feat_axes)
    view_rows = hidden_act[0]
    rows_here = view_rows.shape[0]
    half_rows = rows_here * depth
    row_total = half_rows * lax.axis_size("x_lo")
    feat_here = proj_weight.shape[1]
    own = feat_here // depth
    twin = lax.axis_index("twin")
    projected = project(proj_weight.T, view_rows)
    by_rows = lax.all_to_all(
        projected.reshape(depth, own, rows_here), "z", 0, 0, tiled=True
    )
    sums = jnp.stack(
        [jnp.sum(by_rows, axis=(0, 2)), jnp.sum(by_rows * by_rows, axis=(0, 2))]
    )
    sums = lax.psum(sums, "x_lo")
    feat_mean = (sums[0] / row_total)[None, :, None]
    feat_var = (sums[1] / row_total)[None, :, None] - feat_mean * feat_mean
    normed = ((by_rows - feat_mean) * lax.rsqrt(feat_var + epsilon)).astype(bf16)
    normed = normed.transpose(1, 0, 2).reshape(own, half_rows)
    other = lax.ppermute(normed, "twin", swap)
    there = spread(normed, feat_axes).reshape(feats * own, half_rows)
    here = lax.all_gather(other, "z", axis=0, tiled=True)
    corr = lax.dot_general(
        here, there, (((1,), (1,)), ((), ())), preferred_element_type=f32
    )
    place = jnp.stack(
        [lax.axis_index("z") * own, lax.axis_index(feat_axes) * own, jnp.int32(own)]
    )
    taken = lax.ppermute(pack(place, corr), "x_lo", swap)
    part = products(place, corr, taken, there, rows_here, row_total)
    terms = lax.all_to_all(part, "z", 0, 0, tiled=True)
    total = jnp.sum(terms.astype(f32), axis=0)
    first, second = jnp.split(total, 2, axis=0)
    keep = jnp.where(twin == 0, first, second)
    give = jnp.where(twin == 0, second, first)
    take = lax.ppermute(give, "twin", swap)
    return jnp.stack(
        [jnp.where(twin == 0, take, keep), jnp.where(twin == 0, keep, take)], axis=1
    )


def solution(mesh):
    parts = 2
    shape = mesh.devices.shape
    fine = Mesh(
        mesh.devices.reshape(
            parts, shape[0] // parts, parts, shape[1] // parts, shape[2]
        ),
        ("x_hi", "y", "x_lo", "z", "twin"),
    )
    return jax.shard_map(
        shards,
        mesh=fine,
        in_specs=(P("twin", batch_axes, None), P(None, feat_axes)),
        out_specs=P(feat_axes + ("twin",), None, batch_axes),
        check_vma=False,
    )
```

```python
import functools

import jax
import jax.numpy as jnp
from jax import lax
from jax.experimental import pallas as pl
from jax.experimental.pallas import tpu as pltpu
from jax.sharding import Mesh
from jax.sharding import PartitionSpec as P

epsilon = 1e-05
off_weight = 0.0051
batch_axes = ("x_lo", "z")
feat_axes = ("x_hi", "y")
bf16, f32 = jnp.bfloat16, jnp.float32
swap = [(0, 1), (1, 0)]


def spread(part, axes):
    copies = jnp.broadcast_to(part[None], (lax.axis_size(axes),) + part.shape)
    return lax.all_to_all(copies, axes, 0, 0, tiled=True)


def project_kernel(weight_hbm, rows_hbm, out_ref, weight_ref, rows_ref, sems):
    parts = sems.shape[1]
    width = weight_ref.shape[1] // parts
    copies = []
    for part in range(parts):
        cols = pl.ds(part * width, width)
        pair = [
            pltpu.make_async_copy(
                weight_hbm.at[:, cols], weight_ref.at[:, cols], sems.at[0, part]
            ),
            pltpu.make_async_copy(
                rows_hbm.at[:, cols], rows_ref.at[:, cols], sems.at[1, part]
            ),
        ]
        for copy in pair:
            copy.start()
        copies.append(pair)
    total = None
    for part, pair in enumerate(copies):
        for copy in pair:
            copy.wait()
        cols = slice(part * width, (part + 1) * width)
        term = lax.dot_general(
            weight_ref[:, cols],
            rows_ref[:, cols],
            (((1,), (1,)), ((), ())),
            preferred_element_type=f32,
        )
        total = term if total is None else total + term
    out_ref[...] = total


def project(weight, rows, parts=8):
    return pl.pallas_call(
        project_kernel,
        out_shape=jax.ShapeDtypeStruct((weight.shape[0], rows.shape[0]), f32),
        in_specs=[pl.BlockSpec(memory_space=pl.ANY)] * 2,
        out_specs=pl.BlockSpec(memory_space=pltpu.VMEM),
        scratch_shapes=[
            pltpu.VMEM(weight.shape, bf16),
            pltpu.VMEM(rows.shape, bf16),
            pltpu.SemaphoreType.DMA((2, parts)),
        ],
        compiler_params=pltpu.CompilerParams(vmem_limit_bytes=56 * 2**20),
    )(weight, rows)


def on_diagonal(place_ref, shape):
    rows = lax.broadcasted_iota(jnp.int32, shape, 0)
    cols = lax.broadcasted_iota(jnp.int32, shape, 1)
    top, left, own = place_ref[0], place_ref[1], place_ref[2]
    return (cols - rows == left - top) & (rows >= top) & (rows < top + own)


def pack_kernel(place_ref, corr_ref, packed_ref):
    corr = corr_ref[...]
    feats = corr.shape[0]
    diagonal = jnp.where(on_diagonal(place_ref, corr.shape), corr, 0.0)
    diagonal = jnp.sum(diagonal, axis=0, keepdims=True)
    high = diagonal.astype(bf16).astype(f32)
    middle = (diagonal - high).astype(bf16).astype(f32)
    low = diagonal - high - middle
    extra = packed_ref.shape[0] - feats
    index = lax.broadcasted_iota(jnp.int32, (extra, corr.shape[1]), 0)
    tail = jnp.where(index == 0, high, jnp.where(index == 1, middle, low))
    packed_ref[:feats] = corr.astype(bf16)
    packed_ref[feats:] = jnp.where(index < 3, tail, 0.0).astype(bf16)


def pack(place, corr):
    return pl.pallas_call(
        pack_kernel,
        out_shape=jax.ShapeDtypeStruct((corr.shape[0] + 16, corr.shape[1]), bf16),
        in_specs=[
            pl.BlockSpec(memory_space=pltpu.SMEM),
            pl.BlockSpec(memory_space=pltpu.VMEM),
        ],
        out_specs=pl.BlockSpec(memory_space=pltpu.VMEM),
        compiler_params=pltpu.CompilerParams(vmem_limit_bytes=24 * 2**20),
    )(place, corr)


def product_kernel(row_total, place_ref, corr_ref, taken_ref, other_ref, out_ref):
    feats = corr_ref.shape[0]
    rows_here = out_ref.shape[2]
    diagonal = on_diagonal(place_ref, corr_ref.shape)
    terms = jnp.sum(taken_ref[feats:].astype(f32), axis=0, keepdims=True)
    taken = jnp.where(diagonal, terms, taken_ref[:feats].astype(f32))
    corr = (corr_ref[...] + taken) / row_total
    grad = jnp.where(diagonal, -2.0 * (1.0 - corr), 2.0 * off_weight * corr)
    grad = grad.astype(bf16)
    for block in range(out_ref.shape[0]):
        out_ref[block] = jnp.dot(
            grad,
            other_ref[:, block * rows_here : (block + 1) * rows_here],
            preferred_element_type=f32,
        ).astype(bf16)


def products(place, corr, taken, other, rows_here, row_total):
    blocks = other.shape[1] // rows_here
    return pl.pallas_call(
        functools.partial(product_kernel, row_total),
        out_shape=jax.ShapeDtypeStruct((blocks, corr.shape[0], rows_here), bf16),
        in_specs=[pl.BlockSpec(memory_space=pltpu.SMEM)]
        + [pl.BlockSpec(memory_space=pltpu.VMEM)] * 3,
        out_specs=pl.BlockSpec(memory_space=pltpu.VMEM),
        compiler_params=pltpu.CompilerParams(vmem_limit_bytes=24 * 2**20),
    )(place, corr, taken, other)


def shards(hidden_act, proj_weight):
    depth, feats = lax.axis_size("z"), lax.axis_size(feat_axes)
    view_rows = hidden_act[0]
    rows_here = view_rows.shape[0]
    half_rows = rows_here * depth
    row_total = half_rows * lax.axis_size("x_lo")
    feat_here = proj_weight.shape[1]
    own = feat_here // depth
    twin = lax.axis_index("twin")
    projected = project(proj_weight.T, view_rows)
    by_rows = lax.all_to_all(
        projected.reshape(depth, own, rows_here), "z", 0, 0, tiled=True
    )
    sums = jnp.stack(
        [jnp.sum(by_rows, axis=(0, 2)), jnp.sum(by_rows * by_rows, axis=(0, 2))]
    )
    sums = lax.psum(sums, "x_lo")
    feat_mean = (sums[0] / row_total)[None, :, None]
    feat_var = (sums[1] / row_total)[None, :, None] - feat_mean * feat_mean
    normed = ((by_rows - feat_mean) * lax.rsqrt(feat_var + epsilon)).astype(bf16)
    normed = normed.transpose(1, 0, 2).reshape(own, half_rows)
    far = lax.ppermute(normed, "x_hi", swap)
    other = lax.ppermute(normed, "twin", swap)
    low = lax.axis_index("x_hi") == 0
    pair = jnp.concatenate([jnp.where(low, normed, far), jnp.where(low, far, normed)])
    pair, other = lax.optimization_barrier((pair, other))
    there = spread(pair, "y").reshape(feats * own, half_rows)
    here = lax.all_gather(other, "z", axis=0, tiled=True)
    corr = lax.dot_general(
        here, there, (((1,), (1,)), ((), ())), preferred_element_type=f32
    )
    chunk = lax.axis_index("y") * lax.axis_size("x_hi") + lax.axis_index("x_hi")
    place = jnp.stack(
        [lax.axis_index("z") * own, chunk * own, jnp.int32(own)]
    )
    taken = lax.ppermute(pack(place, corr), "x_lo", swap)
    part = products(place, corr, taken, there, rows_here, row_total)
    terms = lax.all_to_all(part, "z", 0, 0, tiled=True)
    total = jnp.sum(terms.astype(f32), axis=0)
    first, second = jnp.split(total, 2, axis=0)
    keep = jnp.where(twin == 0, first, second)
    give = jnp.where(twin == 0, second, first)
    take = lax.ppermute(give, "twin", swap)
    return jnp.stack(
        [jnp.where(twin == 0, take, keep), jnp.where(twin == 0, keep, take)], axis=1
    )


def solution(mesh):
    parts = 2
    shape = mesh.devices.shape
    fine = Mesh(
        mesh.devices.reshape(
            parts, shape[0] // parts, parts, shape[1] // parts, shape[2]
        ),
        ("x_hi", "y", "x_lo", "z", "twin"),
    )
    return jax.shard_map(
        shards,
        mesh=fine,
        in_specs=(P("twin", batch_axes, None), P(None, feat_axes)),
        out_specs=P(feat_axes + ("twin",), None, batch_axes),
        check_vma=False,
    )
```

```python
import functools

import jax
import jax.numpy as jnp
from jax import lax
from jax.experimental import pallas as pl
from jax.experimental.pallas import tpu as pltpu
from jax.sharding import Mesh
from jax.sharding import PartitionSpec as P

epsilon = 1e-05
off_weight = 0.0051
batch_axes = ("x_lo", "z")
feat_axes = ("x_hi", "y")
bf16, f32 = jnp.bfloat16, jnp.float32
swap = [(0, 1), (1, 0)]


def spread(part, axes):
    copies = jnp.broadcast_to(part[None], (lax.axis_size(axes),) + part.shape)
    return lax.all_to_all(copies, axes, 0, 0, tiled=True)


def trade(part):
    both = lax.all_gather(part, "twin", axis=0, tiled=True)
    first, second = jnp.split(both, 2, axis=0)
    return jnp.where(lax.axis_index("twin") == 0, second, first)


def project_kernel(weight_hbm, rows_hbm, out_ref, weight_ref, rows_ref, sems):
    parts = sems.shape[1]
    width = weight_ref.shape[1] // parts
    copies = []
    for part in range(parts):
        cols = pl.ds(part * width, width)
        pair = [
            pltpu.make_async_copy(
                weight_hbm.at[:, cols], weight_ref.at[:, cols], sems.at[0, part]
            ),
            pltpu.make_async_copy(
                rows_hbm.at[:, cols], rows_ref.at[:, cols], sems.at[1, part]
            ),
        ]
        for copy in pair:
            copy.start()
        copies.append(pair)
    total = None
    for part, pair in enumerate(copies):
        for copy in pair:
            copy.wait()
        cols = slice(part * width, (part + 1) * width)
        term = lax.dot_general(
            weight_ref[:, cols],
            rows_ref[:, cols],
            (((1,), (1,)), ((), ())),
            preferred_element_type=f32,
        )
        total = term if total is None else total + term
    out_ref[...] = total


def project(weight, rows, parts=8):
    return pl.pallas_call(
        project_kernel,
        out_shape=jax.ShapeDtypeStruct((weight.shape[0], rows.shape[0]), f32),
        in_specs=[pl.BlockSpec(memory_space=pl.ANY)] * 2,
        out_specs=pl.BlockSpec(memory_space=pltpu.VMEM),
        scratch_shapes=[
            pltpu.VMEM(weight.shape, bf16),
            pltpu.VMEM(rows.shape, bf16),
            pltpu.SemaphoreType.DMA((2, parts)),
        ],
        compiler_params=pltpu.CompilerParams(vmem_limit_bytes=56 * 2**20),
    )(weight, rows)


def on_diagonal(place_ref, shape):
    rows = lax.broadcasted_iota(jnp.int32, shape, 0)
    cols = lax.broadcasted_iota(jnp.int32, shape, 1)
    top, left, own = place_ref[0], place_ref[1], place_ref[2]
    return (cols - rows == left - top) & (rows >= top) & (rows < top + own)


def pack_kernel(place_ref, corr_ref, packed_ref):
    corr = corr_ref[...]
    feats = corr.shape[0]
    diagonal = jnp.where(on_diagonal(place_ref, corr.shape), corr, 0.0)
    diagonal = jnp.sum(diagonal, axis=0, keepdims=True)
    high = diagonal.astype(bf16).astype(f32)
    middle = (diagonal - high).astype(bf16).astype(f32)
    low = diagonal - high - middle
    extra = packed_ref.shape[0] - feats
    index = lax.broadcasted_iota(jnp.int32, (extra, corr.shape[1]), 0)
    tail = jnp.where(index == 0, high, jnp.where(index == 1, middle, low))
    packed_ref[:feats] = corr.astype(bf16)
    packed_ref[feats:] = jnp.where(index < 3, tail, 0.0).astype(bf16)


def pack(place, corr):
    return pl.pallas_call(
        pack_kernel,
        out_shape=jax.ShapeDtypeStruct((corr.shape[0] + 16, corr.shape[1]), bf16),
        in_specs=[
            pl.BlockSpec(memory_space=pltpu.SMEM),
            pl.BlockSpec(memory_space=pltpu.VMEM),
        ],
        out_specs=pl.BlockSpec(memory_space=pltpu.VMEM),
        compiler_params=pltpu.CompilerParams(vmem_limit_bytes=24 * 2**20),
    )(place, corr)


def product_kernel(row_total, place_ref, corr_ref, taken_ref, other_ref, out_ref):
    feats = corr_ref.shape[0]
    rows_here = out_ref.shape[2]
    diagonal = on_diagonal(place_ref, corr_ref.shape)
    terms = jnp.sum(taken_ref[feats:].astype(f32), axis=0, keepdims=True)
    taken = jnp.where(diagonal, terms, taken_ref[:feats].astype(f32))
    corr = (corr_ref[...] + taken) / row_total
    grad = jnp.where(diagonal, -2.0 * (1.0 - corr), 2.0 * off_weight * corr)
    grad = grad.astype(bf16)
    for block in range(out_ref.shape[0]):
        out_ref[block] = jnp.dot(
            grad,
            other_ref[:, block * rows_here : (block + 1) * rows_here],
            preferred_element_type=f32,
        ).astype(bf16)


def products(place, corr, taken, other, rows_here, row_total):
    blocks = other.shape[1] // rows_here
    return pl.pallas_call(
        functools.partial(product_kernel, row_total),
        out_shape=jax.ShapeDtypeStruct((blocks, corr.shape[0], rows_here), bf16),
        in_specs=[pl.BlockSpec(memory_space=pltpu.SMEM)]
        + [pl.BlockSpec(memory_space=pltpu.VMEM)] * 3,
        out_specs=pl.BlockSpec(memory_space=pltpu.VMEM),
        compiler_params=pltpu.CompilerParams(vmem_limit_bytes=24 * 2**20),
    )(place, corr, taken, other)


def shards(hidden_act, proj_weight):
    depth, feats = lax.axis_size("z"), lax.axis_size(feat_axes)
    view_rows = hidden_act[0]
    rows_here = view_rows.shape[0]
    half_rows = rows_here * depth
    row_total = half_rows * lax.axis_size("x_lo")
    feat_here = proj_weight.shape[1]
    own = feat_here // depth
    twin = lax.axis_index("twin")
    projected = project(proj_weight.T, view_rows)
    by_rows = lax.all_to_all(
        projected.reshape(depth, own, rows_here), "z", 0, 0, tiled=True
    )
    sums = jnp.stack(
        [jnp.sum(by_rows, axis=(0, 2)), jnp.sum(by_rows * by_rows, axis=(0, 2))]
    )
    sums = jnp.sum(lax.all_gather(sums, "x_lo", axis=0), axis=0)
    feat_mean = (sums[0] / row_total)[None, :, None]
    feat_var = (sums[1] / row_total)[None, :, None] - feat_mean * feat_mean
    normed = ((by_rows - feat_mean) * lax.rsqrt(feat_var + epsilon)).astype(bf16)
    normed = normed.transpose(1, 0, 2).reshape(own, half_rows)
    other = trade(normed)
    there = spread(normed, feat_axes).reshape(feats * own, half_rows)
    here = lax.all_gather(other, "z", axis=0, tiled=True)
    corr = lax.dot_general(
        here, there, (((1,), (1,)), ((), ())), preferred_element_type=f32
    )
    place = jnp.stack(
        [lax.axis_index("z") * own, lax.axis_index(feat_axes) * own, jnp.int32(own)]
    )
    taken = lax.ppermute(pack(place, corr), "x_lo", swap)
    part = products(place, corr, taken, there, rows_here, row_total)
    terms = lax.all_to_all(part, "z", 0, 0, tiled=True)
    total = jnp.sum(terms.astype(f32), axis=0)
    first, second = jnp.split(total, 2, axis=0)
    keep = jnp.where(twin == 0, first, second)
    give = jnp.where(twin == 0, second, first)
    take = trade(give)
    return jnp.stack(
        [jnp.where(twin == 0, take, keep), jnp.where(twin == 0, keep, take)], axis=1
    )


def solution(mesh):
    parts = 2
    shape = mesh.devices.shape
    fine = Mesh(
        mesh.devices.reshape(
            parts, shape[0] // parts, parts, shape[1] // parts, shape[2]
        ),
        ("x_hi", "y", "x_lo", "z", "twin"),
    )
    return jax.shard_map(
        shards,
        mesh=fine,
        in_specs=(P("twin", batch_axes, None), P(None, feat_axes)),
        out_specs=P(feat_axes + ("twin",), None, batch_axes),
        check_vma=False,
    )
```

```python
import functools

import jax
import jax.numpy as jnp
from jax import lax
from jax.experimental import pallas as pl
from jax.experimental.pallas import tpu as pltpu
from jax.sharding import Mesh
from jax.sharding import PartitionSpec as P

epsilon = 1e-05
off_weight = 0.0051
depth_axes = ("z_hi", "z_lo")
batch_axes = ("x_lo",) + depth_axes
feat_axes = ("x_hi", "y")
bf16, f32 = jnp.bfloat16, jnp.float32
swap = [(0, 1), (1, 0)]


def spread(part, axes):
    copies = jnp.broadcast_to(part[None], (lax.axis_size(axes),) + part.shape)
    return lax.all_to_all(copies, axes, 0, 0, tiled=True)


def trade(part):
    both = lax.all_gather(part, "twin", axis=0, tiled=True)
    first, second = jnp.split(both, 2, axis=0)
    return jnp.where(lax.axis_index("twin") == 0, second, first)


def project_kernel(weight_hbm, rows_hbm, out_ref, weight_ref, rows_ref, sems):
    parts = sems.shape[1]
    width = weight_ref.shape[1] // parts
    copies = []
    for part in range(parts):
        cols = pl.ds(part * width, width)
        pair = [
            pltpu.make_async_copy(
                weight_hbm.at[:, cols], weight_ref.at[:, cols], sems.at[0, part]
            ),
            pltpu.make_async_copy(
                rows_hbm.at[:, cols], rows_ref.at[:, cols], sems.at[1, part]
            ),
        ]
        for copy in pair:
            copy.start()
        copies.append(pair)
    total = None
    for part, pair in enumerate(copies):
        for copy in pair:
            copy.wait()
        cols = slice(part * width, (part + 1) * width)
        term = lax.dot_general(
            weight_ref[:, cols],
            rows_ref[:, cols],
            (((1,), (1,)), ((), ())),
            preferred_element_type=f32,
        )
        total = term if total is None else total + term
    out_ref[...] = total


def project(weight, rows, parts=8):
    return pl.pallas_call(
        project_kernel,
        out_shape=jax.ShapeDtypeStruct((weight.shape[0], rows.shape[0]), f32),
        in_specs=[pl.BlockSpec(memory_space=pl.ANY)] * 2,
        out_specs=pl.BlockSpec(memory_space=pltpu.VMEM),
        scratch_shapes=[
            pltpu.VMEM(weight.shape, bf16),
            pltpu.VMEM(rows.shape, bf16),
            pltpu.SemaphoreType.DMA((2, parts)),
        ],
        compiler_params=pltpu.CompilerParams(vmem_limit_bytes=56 * 2**20),
    )(weight, rows)


def on_diagonal(place_ref, shape):
    rows = lax.broadcasted_iota(jnp.int32, shape, 0)
    cols = lax.broadcasted_iota(jnp.int32, shape, 1)
    top, left, own = place_ref[0], place_ref[1], place_ref[2]
    return (cols - rows == left - top) & (rows >= top) & (rows < top + own)


def pack_kernel(place_ref, corr_ref, packed_ref):
    corr = corr_ref[...]
    feats = corr.shape[0]
    diagonal = jnp.where(on_diagonal(place_ref, corr.shape), corr, 0.0)
    diagonal = jnp.sum(diagonal, axis=0, keepdims=True)
    high = diagonal.astype(bf16).astype(f32)
    middle = (diagonal - high).astype(bf16).astype(f32)
    low = diagonal - high - middle
    extra = packed_ref.shape[0] - feats
    index = lax.broadcasted_iota(jnp.int32, (extra, corr.shape[1]), 0)
    tail = jnp.where(index == 0, high, jnp.where(index == 1, middle, low))
    packed_ref[:feats] = corr.astype(bf16)
    packed_ref[feats:] = jnp.where(index < 3, tail, 0.0).astype(bf16)


def pack(place, corr):
    return pl.pallas_call(
        pack_kernel,
        out_shape=jax.ShapeDtypeStruct((corr.shape[0] + 16, corr.shape[1]), bf16),
        in_specs=[
            pl.BlockSpec(memory_space=pltpu.SMEM),
            pl.BlockSpec(memory_space=pltpu.VMEM),
        ],
        out_specs=pl.BlockSpec(memory_space=pltpu.VMEM),
        compiler_params=pltpu.CompilerParams(vmem_limit_bytes=24 * 2**20),
    )(place, corr)


def product_kernel(
    row_total, near_count, place_ref, corr_ref, taken_ref, other_ref, out_ref
):
    feats = corr_ref.shape[0]
    rows_here = out_ref.shape[2]
    diagonal = on_diagonal(place_ref, corr_ref.shape)
    terms = jnp.sum(taken_ref[feats:].astype(f32), axis=0, keepdims=True)
    taken = jnp.where(diagonal, terms, taken_ref[:feats].astype(f32))
    corr = (corr_ref[...] + taken) / row_total
    grad = jnp.where(diagonal, -2.0 * (1.0 - corr), 2.0 * off_weight * corr)
    grad = grad.astype(bf16)
    blocks = out_ref.shape[0]
    for block in range(blocks):
        far, near = divmod(block, near_count)
        out_ref[near * (blocks // near_count) + far] = jnp.dot(
            grad,
            other_ref[:, block * rows_here : (block + 1) * rows_here],
            preferred_element_type=f32,
        ).astype(bf16)


def products(place, corr, taken, other, rows_here, row_total, near_count):
    blocks = other.shape[1] // rows_here
    return pl.pallas_call(
        functools.partial(product_kernel, row_total, near_count),
        out_shape=jax.ShapeDtypeStruct((blocks, corr.shape[0], rows_here), bf16),
        in_specs=[pl.BlockSpec(memory_space=pltpu.SMEM)]
        + [pl.BlockSpec(memory_space=pltpu.VMEM)] * 3,
        out_specs=pl.BlockSpec(memory_space=pltpu.VMEM),
        compiler_params=pltpu.CompilerParams(vmem_limit_bytes=24 * 2**20),
    )(place, corr, taken, other)


def shards(hidden_act, proj_weight):
    depth, feats = lax.axis_size(depth_axes), lax.axis_size(feat_axes)
    view_rows = hidden_act[0]
    rows_here = view_rows.shape[0]
    half_rows = rows_here * depth
    row_total = half_rows * lax.axis_size("x_lo")
    feat_here = proj_weight.shape[1]
    own = feat_here // depth
    twin = lax.axis_index("twin")
    projected = project(proj_weight.T, view_rows)
    by_rows = lax.all_to_all(
        projected.reshape(depth, own, rows_here), depth_axes, 0, 0, tiled=True
    )
    sums = jnp.stack(
        [jnp.sum(by_rows, axis=(0, 2)), jnp.sum(by_rows * by_rows, axis=(0, 2))]
    )
    sums = jnp.sum(lax.all_gather(sums, "x_lo", axis=0), axis=0)
    feat_mean = (sums[0] / row_total)[None, :, None]
    feat_var = (sums[1] / row_total)[None, :, None] - feat_mean * feat_mean
    normed = ((by_rows - feat_mean) * lax.rsqrt(feat_var + epsilon)).astype(bf16)
    normed = normed.transpose(1, 0, 2).reshape(own, half_rows)
    other = trade(normed)
    there = spread(normed, feat_axes).reshape(feats * own, half_rows)
    here = lax.all_gather(other, depth_axes, axis=0, tiled=True)
    corr = lax.dot_general(
        here, there, (((1,), (1,)), ((), ())), preferred_element_type=f32
    )
    place = jnp.stack(
        [lax.axis_index(depth_axes) * own, lax.axis_index(feat_axes) * own, jnp.int32(own)]
    )
    taken = lax.ppermute(pack(place, corr), "x_lo", swap)
    near_count = lax.axis_size("z_lo")
    part = products(place, corr, taken, there, rows_here, row_total, near_count)
    terms = lax.all_to_all(part, "z_lo", 0, 0, tiled=True)
    near = terms.reshape((near_count, -1) + terms.shape[1:]).astype(f32)
    near = jnp.sum(near, axis=0).astype(bf16)
    terms = lax.all_to_all(near, "z_hi", 0, 0, tiled=True)
    total = jnp.sum(terms.astype(f32), axis=0)
    first, second = jnp.split(total, 2, axis=0)
    keep = jnp.where(twin == 0, first, second)
    give = jnp.where(twin == 0, second, first)
    take = trade(give)
    return jnp.stack(
        [jnp.where(twin == 0, take, keep), jnp.where(twin == 0, keep, take)], axis=1
    )


def solution(mesh):
    parts = 2
    shape = mesh.devices.shape
    depth = shape[1] // parts
    near = 3 if depth % 3 == 0 else 1
    fine = Mesh(
        mesh.devices.reshape(
            parts, shape[0] // parts, parts, depth // near, near, shape[2]
        ),
        ("x_hi", "y", "x_lo", "z_hi", "z_lo", "twin"),
    )
    return jax.shard_map(
        shards,
        mesh=fine,
        in_specs=(P("twin", batch_axes, None), P(None, feat_axes)),
        out_specs=P(feat_axes + ("twin",), None, batch_axes),
        check_vma=False,
    )
```

```python
import functools

import jax
import jax.numpy as jnp
from jax import lax
from jax.experimental import pallas as pl
from jax.experimental.pallas import tpu as pltpu
from jax.sharding import Mesh
from jax.sharding import PartitionSpec as P

epsilon = 1e-05
off_weight = 0.0051
depth_axes = ("z_hi", "z_lo")
batch_axes = ("x_lo",) + depth_axes
feat_axes = ("x_hi", "y")
bf16, f32 = jnp.bfloat16, jnp.float32
swap = [(0, 1), (1, 0)]


def spread(part, axes):
    copies = jnp.broadcast_to(part[None], (lax.axis_size(axes),) + part.shape)
    return lax.all_to_all(copies, axes, 0, 0, tiled=True)


def trade(part):
    both = lax.all_gather(part, "twin", axis=0, tiled=True)
    first, second = jnp.split(both, 2, axis=0)
    return jnp.where(lax.axis_index("twin") == 0, second, first)


def project_kernel(weight_hbm, rows_hbm, out_ref, weight_ref, rows_ref, sems):
    parts = sems.shape[1]
    width = weight_ref.shape[1] // parts
    copies = []
    for part in range(parts):
        cols = pl.ds(part * width, width)
        pair = [
            pltpu.make_async_copy(
                weight_hbm.at[:, cols], weight_ref.at[:, cols], sems.at[0, part]
            ),
            pltpu.make_async_copy(
                rows_hbm.at[:, cols], rows_ref.at[:, cols], sems.at[1, part]
            ),
        ]
        for copy in pair:
            copy.start()
        copies.append(pair)
    total = None
    for part, pair in enumerate(copies):
        for copy in pair:
            copy.wait()
        cols = slice(part * width, (part + 1) * width)
        term = lax.dot_general(
            weight_ref[:, cols],
            rows_ref[:, cols],
            (((1,), (1,)), ((), ())),
            preferred_element_type=f32,
        )
        total = term if total is None else total + term
    out_ref[...] = total


def project(weight, rows, parts=8):
    return pl.pallas_call(
        project_kernel,
        out_shape=jax.ShapeDtypeStruct((weight.shape[0], rows.shape[0]), f32),
        in_specs=[pl.BlockSpec(memory_space=pl.ANY)] * 2,
        out_specs=pl.BlockSpec(memory_space=pltpu.VMEM),
        scratch_shapes=[
            pltpu.VMEM(weight.shape, bf16),
            pltpu.VMEM(rows.shape, bf16),
            pltpu.SemaphoreType.DMA((2, parts)),
        ],
        compiler_params=pltpu.CompilerParams(vmem_limit_bytes=56 * 2**20),
    )(weight, rows)


def on_diagonal(place_ref, shape):
    rows = lax.broadcasted_iota(jnp.int32, shape, 0)
    cols = lax.broadcasted_iota(jnp.int32, shape, 1)
    top, left, own = place_ref[0], place_ref[1], place_ref[2]
    return (cols - rows == left - top) & (rows >= top) & (rows < top + own)


def pack_kernel(place_ref, corr_ref, packed_ref):
    corr = corr_ref[...]
    feats = corr.shape[0]
    diagonal = jnp.where(on_diagonal(place_ref, corr.shape), corr, 0.0)
    diagonal = jnp.sum(diagonal, axis=0, keepdims=True)
    high = diagonal.astype(bf16).astype(f32)
    middle = (diagonal - high).astype(bf16).astype(f32)
    low = diagonal - high - middle
    extra = packed_ref.shape[0] - feats
    index = lax.broadcasted_iota(jnp.int32, (extra, corr.shape[1]), 0)
    tail = jnp.where(index == 0, high, jnp.where(index == 1, middle, low))
    packed_ref[:feats] = corr.astype(bf16)
    packed_ref[feats:] = jnp.where(index < 3, tail, 0.0).astype(bf16)


def pack(place, corr):
    return pl.pallas_call(
        pack_kernel,
        out_shape=jax.ShapeDtypeStruct((corr.shape[0] + 16, corr.shape[1]), bf16),
        in_specs=[
            pl.BlockSpec(memory_space=pltpu.SMEM),
            pl.BlockSpec(memory_space=pltpu.VMEM),
        ],
        out_specs=pl.BlockSpec(memory_space=pltpu.VMEM),
        compiler_params=pltpu.CompilerParams(vmem_limit_bytes=24 * 2**20),
    )(place, corr)


def product_kernel(
    row_total, near_count, place_ref, corr_ref, taken_ref, other_ref, out_ref
):
    feats = corr_ref.shape[0]
    rows_here = out_ref.shape[2]
    diagonal = on_diagonal(place_ref, corr_ref.shape)
    terms = jnp.sum(taken_ref[feats:].astype(f32), axis=0, keepdims=True)
    taken = jnp.where(diagonal, terms, taken_ref[:feats].astype(f32))
    corr = (corr_ref[...] + taken) / row_total
    grad = jnp.where(diagonal, -2.0 * (1.0 - corr), 2.0 * off_weight * corr)
    grad = grad.astype(bf16)
    blocks = out_ref.shape[0]
    for block in range(blocks):
        far, near = divmod(block, near_count)
        out_ref[near * (blocks // near_count) + far] = jnp.dot(
            grad,
            other_ref[:, block * rows_here : (block + 1) * rows_here],
            preferred_element_type=f32,
        ).astype(bf16)


def products(place, corr, taken, other, rows_here, row_total, near_count):
    blocks = other.shape[1] // rows_here
    return pl.pallas_call(
        functools.partial(product_kernel, row_total, near_count),
        out_shape=jax.ShapeDtypeStruct((blocks, corr.shape[0], rows_here), bf16),
        in_specs=[pl.BlockSpec(memory_space=pltpu.SMEM)]
        + [pl.BlockSpec(memory_space=pltpu.VMEM)] * 3,
        out_specs=pl.BlockSpec(memory_space=pltpu.VMEM),
        compiler_params=pltpu.CompilerParams(vmem_limit_bytes=24 * 2**20),
    )(place, corr, taken, other)


def shards(hidden_act, proj_weight):
    depth, feats = lax.axis_size(depth_axes), lax.axis_size(feat_axes)
    view_rows = hidden_act[0]
    rows_here = view_rows.shape[0]
    half_rows = rows_here * depth
    row_total = half_rows * lax.axis_size("x_lo")
    feat_here = proj_weight.shape[1]
    own = feat_here // depth
    twin = lax.axis_index("twin")
    projected = project(proj_weight.T, view_rows)
    near_count = lax.axis_size("z_lo")
    by_rows = projected.reshape(-1, near_count, own, rows_here)
    by_rows = lax.all_to_all(by_rows, "z_lo", 1, 1, tiled=True)
    by_rows = lax.all_to_all(by_rows, "z_hi", 0, 0, tiled=True)
    by_rows = by_rows.reshape(depth, own, rows_here)
    sums = jnp.stack(
        [jnp.sum(by_rows, axis=(0, 2)), jnp.sum(by_rows * by_rows, axis=(0, 2))]
    )
    sums = jnp.sum(lax.all_gather(sums, "x_lo", axis=0), axis=0)
    feat_mean = (sums[0] / row_total)[None, :, None]
    feat_var = (sums[1] / row_total)[None, :, None] - feat_mean * feat_mean
    normed = ((by_rows - feat_mean) * lax.rsqrt(feat_var + epsilon)).astype(bf16)
    normed = normed.transpose(1, 0, 2).reshape(own, half_rows)
    other = trade(normed)
    there = spread(normed, feat_axes).reshape(feats * own, half_rows)
    here = lax.all_gather(other, depth_axes, axis=0, tiled=True)
    corr = lax.dot_general(
        here, there, (((1,), (1,)), ((), ())), preferred_element_type=f32
    )
    place = jnp.stack(
        [lax.axis_index(depth_axes) * own, lax.axis_index(feat_axes) * own, jnp.int32(own)]
    )
    taken = lax.ppermute(pack(place, corr), "x_lo", swap)
    part = products(place, corr, taken, there, rows_here, row_total, near_count)
    terms = lax.all_to_all(part, "z_lo", 0, 0, tiled=True)
    near = terms.reshape((near_count, -1) + terms.shape[1:]).astype(f32)
    near = jnp.sum(near, axis=0).astype(bf16)
    terms = lax.all_to_all(near, "z_hi", 0, 0, tiled=True)
    total = jnp.sum(terms.astype(f32), axis=0)
    first, second = jnp.split(total, 2, axis=0)
    keep = jnp.where(twin == 0, first, second)
    give = jnp.where(twin == 0, second, first)
    take = trade(give)
    return jnp.stack(
        [jnp.where(twin == 0, take, keep), jnp.where(twin == 0, keep, take)], axis=1
    )


def solution(mesh):
    parts = 2
    shape = mesh.devices.shape
    depth = shape[1] // parts
    near = 3 if depth % 3 == 0 else 1
    fine = Mesh(
        mesh.devices.reshape(
            parts, shape[0] // parts, parts, depth // near, near, shape[2]
        ),
        ("x_hi", "y", "x_lo", "z_hi", "z_lo", "twin"),
    )
    return jax.shard_map(
        shards,
        mesh=fine,
        in_specs=(P("twin", batch_axes, None), P(None, feat_axes)),
        out_specs=P(feat_axes + ("twin",), None, batch_axes),
        check_vma=False,
    )
```

```python
import functools

import jax
import jax.numpy as jnp
from jax import lax
from jax.experimental import pallas as pl
from jax.experimental.pallas import tpu as pltpu
from jax.sharding import Mesh
from jax.sharding import PartitionSpec as P

epsilon = 1e-05
off_weight = 0.0051
depth_axes = ("z_hi", "z_lo")
batch_axes = ("x_lo",) + depth_axes
feat_axes = ("x_hi", "y")
bf16, f32 = jnp.bfloat16, jnp.float32
swap = [(0, 1), (1, 0)]


def spread(part, axes):
    copies = jnp.broadcast_to(part[None], (lax.axis_size(axes),) + part.shape)
    return lax.all_to_all(copies, axes, 0, 0, tiled=True)


def trade(part):
    both = lax.all_gather(part, "twin", axis=0, tiled=True)
    first, second = jnp.split(both, 2, axis=0)
    return jnp.where(lax.axis_index("twin") == 0, second, first)


def project_kernel(weight_hbm, rows_hbm, out_ref, weight_ref, rows_ref, sems):
    parts = sems.shape[1]
    width = weight_ref.shape[1] // parts
    copies = []
    for part in range(parts):
        cols = pl.ds(part * width, width)
        pair = [
            pltpu.make_async_copy(
                weight_hbm.at[:, cols], weight_ref.at[:, cols], sems.at[0, part]
            ),
            pltpu.make_async_copy(
                rows_hbm.at[:, cols], rows_ref.at[:, cols], sems.at[1, part]
            ),
        ]
        for copy in pair:
            copy.start()
        copies.append(pair)
    total = None
    for part, pair in enumerate(copies):
        for copy in pair:
            copy.wait()
        cols = slice(part * width, (part + 1) * width)
        term = lax.dot_general(
            weight_ref[:, cols],
            rows_ref[:, cols],
            (((1,), (1,)), ((), ())),
            preferred_element_type=f32,
        )
        total = term if total is None else total + term
    out_ref[...] = total


def project(weight, rows, parts=8):
    return pl.pallas_call(
        project_kernel,
        out_shape=jax.ShapeDtypeStruct((weight.shape[0], rows.shape[0]), f32),
        in_specs=[pl.BlockSpec(memory_space=pl.ANY)] * 2,
        out_specs=pl.BlockSpec(memory_space=pltpu.VMEM),
        scratch_shapes=[
            pltpu.VMEM(weight.shape, bf16),
            pltpu.VMEM(rows.shape, bf16),
            pltpu.SemaphoreType.DMA((2, parts)),
        ],
        compiler_params=pltpu.CompilerParams(vmem_limit_bytes=56 * 2**20),
    )(weight, rows)


def on_diagonal(place_ref, shape):
    rows = lax.broadcasted_iota(jnp.int32, shape, 0)
    cols = lax.broadcasted_iota(jnp.int32, shape, 1)
    top, left, own = place_ref[0], place_ref[1], place_ref[2]
    return (cols - rows == left - top) & (rows >= top) & (rows < top + own)


def pack_kernel(place_ref, corr_ref, packed_ref):
    corr = corr_ref[...]
    feats = corr.shape[0]
    diagonal = jnp.where(on_diagonal(place_ref, corr.shape), corr, 0.0)
    diagonal = jnp.sum(diagonal, axis=0, keepdims=True)
    high = diagonal.astype(bf16).astype(f32)
    middle = (diagonal - high).astype(bf16).astype(f32)
    low = diagonal - high - middle
    extra = packed_ref.shape[0] - feats
    index = lax.broadcasted_iota(jnp.int32, (extra, corr.shape[1]), 0)
    tail = jnp.where(index == 0, high, jnp.where(index == 1, middle, low))
    packed_ref[:feats] = corr.astype(bf16)
    packed_ref[feats:] = jnp.where(index < 3, tail, 0.0).astype(bf16)


def pack(place, corr):
    return pl.pallas_call(
        pack_kernel,
        out_shape=jax.ShapeDtypeStruct((corr.shape[0] + 16, corr.shape[1]), bf16),
        in_specs=[
            pl.BlockSpec(memory_space=pltpu.SMEM),
            pl.BlockSpec(memory_space=pltpu.VMEM),
        ],
        out_specs=pl.BlockSpec(memory_space=pltpu.VMEM),
        compiler_params=pltpu.CompilerParams(vmem_limit_bytes=24 * 2**20),
    )(place, corr)


def product_kernel(
    row_total, near_count, place_ref, corr_ref, taken_ref, other_ref, out_ref
):
    feats = corr_ref.shape[0]
    rows_here = out_ref.shape[2]
    diagonal = on_diagonal(place_ref, corr_ref.shape)
    terms = jnp.sum(taken_ref[feats:].astype(f32), axis=0, keepdims=True)
    taken = jnp.where(diagonal, terms, taken_ref[:feats].astype(f32))
    corr = (corr_ref[...] + taken) / row_total
    grad = jnp.where(diagonal, -2.0 * (1.0 - corr), 2.0 * off_weight * corr)
    grad = grad.astype(bf16)
    blocks = out_ref.shape[0]
    for block in range(blocks):
        far, near = divmod(block, near_count)
        out_ref[near * (blocks // near_count) + far] = jnp.dot(
            grad,
            other_ref[:, block * rows_here : (block + 1) * rows_here],
            preferred_element_type=f32,
        ).astype(bf16)


def products(place, corr, taken, other, rows_here, row_total, near_count):
    blocks = other.shape[1] // rows_here
    return pl.pallas_call(
        functools.partial(product_kernel, row_total, near_count),
        out_shape=jax.ShapeDtypeStruct((blocks, corr.shape[0], rows_here), bf16),
        in_specs=[pl.BlockSpec(memory_space=pltpu.SMEM)]
        + [pl.BlockSpec(memory_space=pltpu.VMEM)] * 3,
        out_specs=pl.BlockSpec(memory_space=pltpu.VMEM),
        compiler_params=pltpu.CompilerParams(vmem_limit_bytes=24 * 2**20),
    )(place, corr, taken, other)


def shards(hidden_act, proj_weight):
    depth, feats = lax.axis_size(depth_axes), lax.axis_size(feat_axes)
    view_rows = hidden_act[0]
    rows_here = view_rows.shape[0]
    half_rows = rows_here * depth
    row_total = half_rows * lax.axis_size("x_lo")
    feat_here = proj_weight.shape[1]
    own = feat_here // depth
    twin = lax.axis_index("twin")
    projected = project(proj_weight.T, view_rows)
    by_rows = lax.all_to_all(
        projected.reshape(depth, own, rows_here), depth_axes, 0, 0, tiled=True
    )
    sums = jnp.stack(
        [jnp.sum(by_rows, axis=(0, 2)), jnp.sum(by_rows * by_rows, axis=(0, 2))]
    )
    sums = jnp.sum(lax.all_gather(sums, "x_lo", axis=0), axis=0)
    feat_mean = (sums[0] / row_total)[None, :, None]
    feat_var = (sums[1] / row_total)[None, :, None] - feat_mean * feat_mean
    normed = ((by_rows - feat_mean) * lax.rsqrt(feat_var + epsilon)).astype(bf16)
    normed = normed.transpose(1, 0, 2).reshape(own, half_rows)
    other = trade(normed)
    there = spread(normed, feat_axes).reshape(feats * own, half_rows)
    here = lax.all_gather(other, depth_axes, axis=0, tiled=True)
    corr = lax.dot_general(
        here, there, (((1,), (1,)), ((), ())), preferred_element_type=f32
    )
    place = jnp.stack(
        [lax.axis_index(depth_axes) * own, lax.axis_index(feat_axes) * own, jnp.int32(own)]
    )
    taken = lax.ppermute(pack(place, corr), "x_lo", swap)
    near_count = lax.axis_size("z_lo")
    part = products(place, corr, taken, there, rows_here, row_total, near_count)
    terms = lax.all_to_all(part, "z_lo", 0, 0, tiled=True)
    near = terms.reshape((near_count, -1) + terms.shape[1:]).astype(f32)
    near = jnp.sum(near, axis=0).astype(bf16)
    terms = lax.all_to_all(near, "z_hi", 0, 0, tiled=True)
    total = jnp.sum(terms.astype(f32), axis=0)
    first, second = jnp.split(total, 2, axis=0)
    keep = jnp.where(twin == 0, first, second)
    give = jnp.where(twin == 0, second, first)
    take = trade(give)
    return jnp.stack(
        [jnp.where(twin == 0, take, keep), jnp.where(twin == 0, keep, take)], axis=1
    )


def solution(mesh):
    parts = 2
    shape = mesh.devices.shape
    depth = shape[1] // parts
    near = 4 if depth % 4 == 0 else 1
    fine = Mesh(
        mesh.devices.reshape(
            parts, shape[0] // parts, parts, depth // near, near, shape[2]
        ),
        ("x_hi", "y", "x_lo", "z_hi", "z_lo", "twin"),
    )
    return jax.shard_map(
        shards,
        mesh=fine,
        in_specs=(P("twin", batch_axes, None), P(None, feat_axes)),
        out_specs=P(feat_axes + ("twin",), None, batch_axes),
        check_vma=False,
    )
```
